512 devices in a mesh: ctx: 64 (over x, y_lo, z), tp: 8 (over y_hi, core).
Axes of the slice: x: 4, y: 8 (y_hi: 4, y_lo: 2; y = y_hi * 2 + y_lo), z: 8, core: 2. Of those that a mesh axis runs over, the one named last changes fastest.
Arguments:
- queries: bfloat16 [8192, 5120], P('ctx', 'tp'), may hold values from -8 to 8
- keys: bfloat16 [16384, 1024], P('ctx', 'tp'), may hold values from -8 to 8
- values: bfloat16 [16384, 1024], P('ctx', 'tp'), may hold values from -6 to 6
- subtree_ends: int32 [16384], P('ctx'), may hold values from 1 to 16384, as said below
- query_positions: int32 [8192], P('ctx'), may hold values from 0 to 16383, as said below
- balance_route: int32 [64, 128], P('ctx'), may hold values from 0 to 127, each once within a row
- out_weight: bfloat16 [5120, 2560], P('tp'), may hold values from -0.3125 to 0.3125
Outputs:
- mixed: bfloat16 [8192, 2560], P(('ctx', 'tp'))
The draws below stay inside these ranges and needn't reach their ends.
Inputs may be any that keep to these rules, and one draw needn't show every extreme that they name: Tokens are packed depth first: for every token k, each token j with k < j < subtree_ends[k] lies in the subtree of k, and subtree_ends[k] > k; token 0 is the root and subtree_ends[0] = 16384. `query_positions`: strictly increasing; query row i stands for a token among positions i * (2) to (i + 1) * 2 - 1. Each row is a permutation of 0 to 127: query row r of the device at ctx index s goes to owner balance_route[s, r] // 2, slot balance_route[s, r] % 2.
All inputs are finite; a program needn't handle non-finite values.
Results may differ from the reference program's by a relative error of at most 0.019.
Values may be sent and summed in bfloat16 or wider, within the bound.
A program may use at most 64 MiB of HBM per device.

```python
import math
import jax
import jax.numpy as jnp
from jax import lax

QUERY_HEADS = 40
KEY_VALUE_HEADS = 8
HEAD_SIZE = 128
DOUT = 2560
Q_DEV = 128
SEND = 2
TREE_TOKENS = 16384
SLAB_QUERIES = 8192
N_CTX = 64


def draw_queries(key, part):
    key = jax.random.fold_in(key, 3)
    first = jax.random.fold_in(key, 0)
    base_offset = jnp.clip(1.5 * jax.random.normal(first, (SLAB_QUERIES, QUERY_HEADS * HEAD_SIZE), jnp.float32), -8.0, 8.0)
    return base_offset.astype(jnp.bfloat16)


def draw_keys(key, part):
    key = jax.random.fold_in(key, 5)
    base_offset = jnp.clip(1.5 * jax.random.normal(key, (TREE_TOKENS, KEY_VALUE_HEADS * HEAD_SIZE), jnp.float32), -8.0, 8.0)
    return base_offset.astype(jnp.bfloat16)


def draw_subtree_ends(key, part):
    key = jax.random.fold_in(key, 7)
    first, second = jax.random.split(key)
    branching = jax.random.randint(first, (TREE_TOKENS,), 0, TREE_TOKENS) < 16
    targets = jax.random.randint(second, (TREE_TOKENS,), 0, 1 << 30)
    slot_index = jnp.arange(TREE_TOKENS, dtype=jnp.int32)

    def descend(depth, inputs):
        position, jump, target = inputs
        jump = jump & (position >= 8)
        back = 2 + target % jnp.maximum(depth - 1, 1)
        level = jnp.where(jump, back, depth + 1)
        return (level, level)
    unused, depths = lax.scan(descend, jnp.int32(-1), (slot_index, branching, targets))
    levels = jnp.arange(TREE_TOKENS, dtype=jnp.int32)

    def climb(nearest, inputs):
        position, depth = inputs
        found = jnp.min(jnp.where(levels <= depth, nearest, TREE_TOKENS))
        nearest = nearest.at[depth].set(position)
        return (nearest, found)
    unused, found = lax.scan(climb, jnp.full((TREE_TOKENS,), TREE_TOKENS, jnp.int32), (slot_index, depths), reverse=True)
    return found.astype(jnp.int32)


def draw_query_positions(key, part):
    key = jax.random.fold_in(key, 9)
    stride = TREE_TOKENS // SLAB_QUERIES
    offsets = jax.random.randint(key, (SLAB_QUERIES,), 0, stride)
    offsets = offsets.at[0].set(0).at[SLAB_QUERIES - 1].set(stride - 1)
    return (jnp.arange(SLAB_QUERIES, dtype=jnp.int32) * stride + offsets).astype(jnp.int32)


def block_levels(key, shape, cuts, least, high):
    def one(axis_at, parts):
        steps = jax.random.uniform(jax.random.fold_in(jax.random.fold_in(key, 6), axis_at), (parts,), jnp.float32, least / len(cuts), high / len(cuts))
        return jnp.repeat(jnp.exp(steps), shape[axis_at] // parts).reshape((-1,) + (1,) * (len(shape) - axis_at - 1))

    gain = one(*cuts[0])
    for cut in cuts[1:]:
        gain = gain * one(*cut)
    return gain


def centred(own_key, dims, spread, limit, cuts=(), held_as=jnp.bfloat16):
    gain = block_levels(own_key, dims, cuts, -0.22, 0.18) if cuts else 1.0
    entries = jax.random.normal(own_key, dims, jnp.float32) * spread * gain
    return jnp.minimum(jnp.maximum(entries, -limit), limit).astype(held_as)


def setup_inputs(seed: int = 0) -> dict:
    arg_keys = jax.random.split(jax.random.key(seed), 8)
    queries = draw_queries(jax.random.fold_in(arg_keys[7], 71), 0)
    keys = draw_keys(jax.random.fold_in(arg_keys[7], 71), 0)
    values = centred(arg_keys[2], (TREE_TOKENS, KEY_VALUE_HEADS * HEAD_SIZE), 1.0, 6.0, ((0, 64), (1, 8)))
    subtree_ends = draw_subtree_ends(jax.random.fold_in(arg_keys[7], 71), 0)
    query_positions = draw_query_positions(jax.random.fold_in(arg_keys[7], 71), 0)
    balance_route = jax.vmap(lambda own: jax.random.permutation(own, Q_DEV))(jax.random.split(arg_keys[5], N_CTX)).reshape((N_CTX, Q_DEV)).astype(jnp.int32)
    out_weight = centred(arg_keys[6], (QUERY_HEADS * HEAD_SIZE, DOUT), (QUERY_HEADS * HEAD_SIZE // 16) ** -0.5, 0.3125, ((0, 8),))
    return {"queries": queries, "keys": keys, "values": values, "subtree_ends": subtree_ends, "query_positions": query_positions, "balance_route": balance_route, "out_weight": out_weight}


def reference(queries, keys, values, subtree_ends, query_positions, balance_route, out_weight):
    query_group = QUERY_HEADS // KEY_VALUE_HEADS
    scale = 1.0 / math.sqrt(HEAD_SIZE)
    current_block = math.gcd(SLAB_QUERIES, 512)
    block_list = SLAB_QUERIES // current_block
    key_index = jnp.arange(TREE_TOKENS, dtype=jnp.int32)

    def single_block(slot_index):
        which_owner = (slot_index // KEY_VALUE_HEADS).astype(jnp.int32)
        current_head = (slot_index % KEY_VALUE_HEADS).astype(jnp.int32)
        zero = jnp.int32(0)
        rows = lax.dynamic_slice(queries, (which_owner * current_block, current_head * query_group * HEAD_SIZE), (current_block, query_group * HEAD_SIZE))
        rows = rows.astype(jnp.float32).reshape(current_block, query_group, HEAD_SIZE)
        key_rows = lax.dynamic_slice(keys, (zero, current_head * HEAD_SIZE), (TREE_TOKENS, HEAD_SIZE)).astype(jnp.float32)
        value_rows = lax.dynamic_slice(values, (zero, current_head * HEAD_SIZE), (TREE_TOKENS, HEAD_SIZE)).astype(jnp.float32)
        positions = lax.dynamic_slice(query_positions, (which_owner * current_block,), (current_block,))
        visible = (key_index[None, :] <= positions[:, None]) & (positions[:, None] < subtree_ends[None, :])
        scores = jnp.einsum('qrd,kd->qrk', rows, key_rows) * scale
        scores = jnp.where(visible[:, None, :], scores, -jnp.inf)
        highest = lax.optimization_barrier(jnp.max(scores, axis=-1, keepdims=True))
        weights = jnp.exp(scores - highest)
        total = lax.optimization_barrier(jnp.sum(weights, axis=-1))
        probs = lax.optimization_barrier(weights.astype(jnp.bfloat16)).astype(jnp.float32)
        output = jnp.einsum('qrk,kd->qrd', probs, value_rows) / total[..., None]
        return output.reshape(current_block, query_group * HEAD_SIZE).astype(jnp.bfloat16)
    piece_list = lax.map(single_block, jnp.arange(block_list * KEY_VALUE_HEADS, dtype=jnp.int32))
    attended_output = piece_list.reshape(block_list, KEY_VALUE_HEADS, current_block, query_group * HEAD_SIZE).transpose(0, 2, 1, 3).reshape(SLAB_QUERIES, QUERY_HEADS * HEAD_SIZE)
    slots = jnp.broadcast_to(jnp.arange(Q_DEV, dtype=jnp.int32), (N_CTX, Q_DEV))
    devices = jnp.broadcast_to(jnp.arange(N_CTX, dtype=jnp.int32)[:, None], (N_CTX, Q_DEV))
    inverse = jnp.zeros((N_CTX, Q_DEV), jnp.int32).at[devices, balance_route].set(slots)
    source = jnp.arange(N_CTX, dtype=jnp.int32)[:, None, None] * Q_DEV + inverse.reshape(N_CTX, N_CTX, SEND)
    source = source.transpose(1, 0, 2).reshape(SLAB_QUERIES)
    moved = jnp.take(attended_output, source, axis=0)
    return jnp.dot(moved, out_weight, preferred_element_type=jnp.float32).astype(jnp.bfloat16)
```

```python
import functools
import math

import jax
import jax.numpy as jnp
from jax import lax
from jax.experimental import pallas as pl
from jax.experimental.pallas import tpu as pltpu
from jax.sharding import PartitionSpec as P

D = 128
HEADS = 5
QW = HEADS * D
NG = 8
NZ = 8
NT = 8
KH = 128
CR = 2 * KH + 16
QR = QW + 16
OW = QW + D
DOUT = 2560
SCALE = math.log2(math.e) / math.sqrt(D)
MASKED = -1e30
START = -1e20
MESH = pl.DeviceIdType.MESH
BF = jnp.bfloat16
F32 = jnp.float32
SPLIT = 3


def digits_row(high, low):
    rows = lax.broadcasted_iota(jnp.int32, (16, D), 0)
    both = jnp.where(rows == 0, jnp.broadcast_to(high, (16, D)), 0)
    both = jnp.where(rows == 1, jnp.broadcast_to(low, (16, D)), both)
    return both.astype(F32).astype(BF)


def kernel(
    q_ref, k_ref, v_ref, i_ref, w_ref, out_ref,
    qt, kv, stage, acc, mx, sm, osend, orecv, att, w_v, part, crecv, ysend, yrecv, zsend, zrecv, fin,
    w_sem, qs, qr, ss, sr, rs, rr, os_, or_, cs, cr, ys, yr, zs, zr,
):
    c, t = lax.axis_index("ctx"), lax.axis_index("tp")
    g, z = c // NZ, c % NZ
    gx, gy = g // 2, g % 2
    th, tc = t // 2, t % 2
    side = g // 4
    low_g = jnp.minimum(g, NG - 1 - g)
    high_g = NG - 1 - low_g
    mate = NG - 1 - g

    def at(group, ring):
        return (group * NZ + ring, t)

    def plane(k):
        step = k // 2
        hop = step + (step // 2) * (1 - 2 * (step % 2))
        return hop, k % 2

    def ahead(k):
        hop, other = plane(k)
        return ((gx + hop) % 4) * 2 + (gy + other) % 2

    def behind(k):
        hop, other = plane(k)
        return ((gx + 4 - hop) % 4) * 2 + (gy + other) % 2

    def remote(src, dst, send, recv, target):
        return pltpu.make_async_remote_copy(
            src_ref=src, dst_ref=dst, send_sem=send, recv_sem=recv, device_id=target, device_id_type=MESH
        )

    w_copy = pltpu.make_async_copy(w_ref, w_v, w_sem)
    w_copy.start()

    barrier = pltpu.get_barrier_semaphore()
    for k in range(1, NG):
        pl.semaphore_signal(barrier, inc=1, device_id=at((g + k) % NG, z), device_id_type=MESH)
    for k in range(1, NZ):
        pl.semaphore_signal(barrier, inc=1, device_id=at(g, (z + k) % NZ), device_id_type=MESH)
    pl.semaphore_signal(barrier, inc=1, device_id=(c, th * 2 + 1 - tc), device_id_type=MESH)
    for k in range(1, 4):
        pl.semaphore_signal(barrier, inc=1, device_id=(c, ((th + k) % 4) * 2 + tc), device_id_type=MESH)

    for half in range(2):
        keys = k_ref[half * KH : (half + 1) * KH, :]
        ends = i_ref[half : half + 1, :]
        ends = digits_row(ends // 128, ends % 128)
        turned = v_ref[half * KH : (half + 1) * KH, :].astype(F32).T.astype(BF)

        def put(ref, keys=keys, ends=ends, turned=turned):
            ref[0:KH, :] = keys
            ref[KH : KH + 16, :] = ends
            ref[KH + 16 :, :] = turned

        @pl.when(side == half)
        def _():
            put(kv.at[side, 0])

        @pl.when(side != half)
        def _():
            put(stage)

    pick = lax.broadcasted_iota(jnp.int32, (D, D), 0) == jnp.broadcast_to(i_ref[3:4, :], (D, D))
    pick = jnp.where(pick, 1.0, 0.0).astype(BF)
    placed = jnp.dot(pick, q_ref[...], preferred_element_type=F32)
    for h in range(HEADS):
        qt[g, h * D : (h + 1) * D, :] = placed[:, h * D : (h + 1) * D].T.astype(BF)
    pos = i_ref[2:3, :]
    pos = digits_row(pos // 128, pos % 128)
    qt[g, QW:, :] = lax.dot_general(pos, pick, (((1,), (1,)), ((), ())), preferred_element_type=F32).astype(BF)

    pl.semaphore_wait(barrier, (NG - 1) + (NZ - 1) + 1 + 3)

    swap = remote(stage, kv.at[side, 0], ss, sr, at(mate, z))
    swap.start()

    right, left = at(g, (z + 1) % NZ), at(g, (z + NZ - 1) % NZ)

    def ring(e, step):
        lane = side if e == 0 else 1 - side
        a, b = (0, 0) if step == 1 else (2 * step - 3, 2 * step - 2)
        if step < 4:
            return (
                remote(kv.at[lane, a], kv.at[lane, 2 * step - 1], rs.at[e, 2 * step - 2], rr.at[e, 2 * step - 2], right),
                remote(kv.at[lane, b], kv.at[lane, 2 * step], rs.at[e, 2 * step - 1], rr.at[e, 2 * step - 1], left),
            )
        cut = KH + 16
        return (
            remote(kv.at[lane, a, 0:cut], kv.at[lane, 7, 0:cut], rs.at[e, 6], rr.at[e, 6], right),
            remote(kv.at[lane, b, cut:CR], kv.at[lane, 7, cut:CR], rs.at[e, 7], rr.at[e, 7], left),
        )

    rings = [[ring(e, step) for step in range(1, 5)] for e in range(2)]

    def launch(e, step):
        if step > 1:
            for copy in rings[e][step - 2]:
                copy.wait_recv()
        elif e == 1:
            swap.wait_recv()
        for copy in rings[e][step - 1]:
            copy.start()

    def query_copy(k):
        return remote(qt.at[g], qt.at[g], qs.at[k], qr.at[k], at(behind(k), z))

    def lower(group):
        return jnp.minimum(group, NG - 1 - group)

    launch(0, 1)
    for k in range(1, NG):

        @pl.when(lower(behind(k)) <= g)
        def _():
            query_copy(k).start()

    launch(1, 1)

    acc[...] = jnp.zeros_like(acc)
    sm[...] = jnp.zeros_like(sm)
    mx[...] = jnp.full_like(mx, START)

    def slot_z(slot):
        hop = (slot + 1) // 2
        return (z + (NZ - hop if slot % 2 else hop)) % NZ

    def flash(b, e, first, last):
        group = low_g if e == 0 else high_g
        row = qt[b, QW : QW + 16, :].astype(F32)
        where = row[0:1, :] * 128.0 + row[1:2, :]
        bias, keys, turned = [], [], []
        for slot in range(first, last):
            ends = kv[e, slot, KH : KH + 16, :].astype(F32)
            ends = jnp.broadcast_to(ends[0:1, :] * 128.0 + ends[1:2, :], (KH, KH)).T
            start = (group * NZ + slot_z(slot)) * (2 * KH) + side * KH
            token = (lax.broadcasted_iota(jnp.int32, (KH, D), 0) + start).astype(F32)
            bias.append(jnp.where((token <= where) & (where < ends), 0.0, MASKED))
            keys.append(kv[e, slot, 0:KH, :])
            turned.append(kv[e, slot, KH + 16 :, :])
        bias, keys, turned = jnp.concatenate(bias, 0), jnp.concatenate(keys, 0), jnp.concatenate(turned, 1)
        for h in range(HEADS):
            cols = slice(h * D, (h + 1) * D)
            s = jnp.dot(keys, qt[b, cols, :], preferred_element_type=F32) + bias
            old = mx[b, 0:1, cols]
            new = jnp.maximum(old, jnp.max(s, axis=0, keepdims=True))
            factor = jnp.exp2((old - new) * SCALE)
            p = jnp.exp2((s - new) * SCALE)
            sm[b, 0:1, cols] = sm[b, 0:1, cols] * factor + jnp.sum(p, axis=0, keepdims=True)
            o = jnp.dot(turned, p.astype(BF), preferred_element_type=F32)
            acc[b, :, cols] = acc[b, :, cols] * factor + o
            mx[b, 0:1, cols] = new

    def first_pass(k, _):
        b = ahead(k)

        @pl.when(b >= low_g)
        def _():
            @pl.when(k > 0)
            def _():
                remote(qt.at[b], qt.at[b], qs.at[k], qr.at[k], at(b, z)).wait_recv()

            flash(b, 0, 0, SPLIT)

        @pl.when(b >= high_g)
        def _():
            flash(b, 1, 0, SPLIT)

        return 0

    launch(0, 2)
    launch(1, 2)
    lax.fori_loop(0, 3, first_pass, 0)
    launch(0, 3)
    launch(1, 3)
    lax.fori_loop(3, 6, first_pass, 0)
    launch(0, 4)
    launch(1, 4)
    lax.fori_loop(6, 8, first_pass, 0)
    for e in range(2):
        for copy in rings[e][3]:
            copy.wait_recv()

    def out_copy(b, k):
        to = (g + k) % NG
        rows = pl.ds(pl.multiple_of(to * 16, 16), 16)
        return remote(osend.at[b, rows], orecv.at[g, b], os_.at[b, k], or_.at[g, b], at(to, z))

    def second_pass(i, _):
        b = NG - 1 - i

        @pl.when(b >= low_g)
        def _():
            flash(b, 0, SPLIT, NZ)

        @pl.when(b >= high_g)
        def _():
            flash(b, 1, SPLIT, NZ)

        @pl.when(b >= low_g)
        def _():
            stats = []
            for h in range(HEADS):
                cols = slice(h * D, (h + 1) * D)
                total = sm[b, 0:1, cols]
                some = total > 0.0
                safe = jnp.where(some, total, 1.0)
                osend[b, :, cols] = (acc[b, :, cols] / safe).T.astype(BF)
                stats.append(jnp.where(some, mx[b, 0:1, cols] * SCALE + jnp.log2(safe), START))
            lse = jnp.concatenate(stats + [jnp.zeros((8 - HEADS, D), F32)], 0)
            one = lse.astype(BF).astype(F32)
            two = (lse - one).astype(BF).astype(F32)
            three = lse - one - two
            table = jnp.concatenate([one, two, three, jnp.zeros((D - 24, D), F32)], 0)
            osend[b, :, QW:] = table.T.astype(BF)
            for k in range(1, NG):
                out_copy(b, k).start()
            orecv[g, b] = osend[b, pl.ds(pl.multiple_of(g * 16, 16), 16), :]

        return 0

    lax.fori_loop(0, NG, second_pass, 0)

    for b in range(NG):
        sources = [s for s in range(NG) if min(s, NG - 1 - s) <= b]
        lses = []
        for s in sources:

            @pl.when(g != s)
            def _():
                remote(orecv.at[s, b], orecv.at[s, b], os_.at[b, 0], or_.at[s, b], at(s, z)).wait_recv()

            digits = orecv[s, b, :, QW:].astype(F32)
            lses.append(digits + pltpu.roll(digits, D - 8, 1) + pltpu.roll(digits, D - 16, 1))
        best = functools.reduce(jnp.maximum, lses)
        weights = [jnp.exp2(lse - best) for lse in lses]
        total = functools.reduce(jnp.add, weights)
        weights = [w / total for w in weights]
        for h in range(HEADS):
            cols = slice(h * D, (h + 1) * D)
            mixed = jnp.zeros((16, D), F32)
            for s, w in zip(sources, weights):
                mixed = mixed + orecv[s, b, :, cols].astype(F32) * w[:, h : h + 1]
            att[b * 16 : (b + 1) * 16, cols] = mixed.astype(BF)

    w_copy.wait()
    for n in range(DOUT // 512):
        cols = slice(n * 512, (n + 1) * 512)
        part[:, cols] = jnp.dot(att[...], w_v[:, cols], preferred_element_type=F32).astype(BF)

    def rows_of(high, core):
        return pl.ds(pl.multiple_of((high * 2 + core) * 16, 16), 16)

    core = [
        remote(part.at[rows_of(j, 1 - tc)], crecv.at[j], cs.at[j], cr.at[j], (c, th * 2 + 1 - tc)) for j in range(4)
    ]
    for copy in core:
        copy.start()
    along = []
    for j in range(4):
        core[j].wait_recv()
        both = part[rows_of(j, tc), :].astype(F32) + crecv[j].astype(F32)

        ysend[j] = both.astype(BF)

        def across(j=j):
            return remote(ysend.at[j], yrecv.at[th], ys.at[j], yr.at[th], (c, j * 2 + tc))

        along.append(across)

        @pl.when(th != j)
        def _():
            across().start()

        @pl.when(th == j)
        def _():
            yrecv[th] = both.astype(BF)

    for j in range(4):

        @pl.when(th != j)
        def _():
            remote(yrecv.at[j], yrecv.at[j], ys.at[j], yr.at[j], (c, j * 2 + tc)).wait_recv()

    total = yrecv[0].astype(F32) + yrecv[1].astype(F32) + yrecv[2].astype(F32) + yrecv[3].astype(F32)
    fin[...] = total
    for j in range(NZ):
        zsend[j] = fin[2 * j : 2 * j + 2, :]
    last = []
    for k in range(1, NZ):
        to = (z + k) % NZ
        copy = remote(zsend.at[to], zrecv.at[z], zs.at[k], zr.at[k], at(g, to))
        copy.start()
        last.append(copy)
    zrecv[z] = zsend[z]
    for copy in last:
        copy.wait_recv()
    for j in range(NZ):
        fin[2 * j : 2 * j + 2, :] = zrecv[j]
    out_ref[...] = fin[...].astype(BF)

    swap.wait_send()
    for e in range(2):
        for pair in rings[e]:
            for copy in pair:
                copy.wait_send()
    for k in range(1, NG):

        @pl.when(lower(behind(k)) <= g)
        def _():
            query_copy(k).wait_send()

    for b in range(NG):

        @pl.when(b >= low_g)
        def _():
            for k in range(1, NG):
                out_copy(b, k).wait_send()

    for copy in core:
        copy.wait_send()
    for j in range(4):

        @pl.when(th != j)
        def _():
            along[j]().wait_send()

    for copy in last:
        copy.wait_send()


def per_device(queries, keys, values, subtree_ends, query_positions, balance_route, out_weight):
    small = jnp.concatenate(
        [
            subtree_ends.reshape(2, D),
            query_positions.reshape(1, D),
            balance_route.reshape(1, D),
            jnp.zeros((4, D), jnp.int32),
        ],
        axis=0,
    )
    vmem = pl.BlockSpec(memory_space=pltpu.VMEM)
    dma = pltpu.SemaphoreType.DMA
    return pl.pallas_call(
        kernel,
        out_shape=jax.ShapeDtypeStruct((16, DOUT), BF),
        in_specs=[vmem, vmem, vmem, vmem, pl.BlockSpec(memory_space=pl.ANY)],
        out_specs=vmem,
        scratch_shapes=[
            pltpu.VMEM((NG, QR, D), BF),
            pltpu.VMEM((2, NZ, CR, D), BF),
            pltpu.VMEM((CR, D), BF),
            pltpu.VMEM((NG, D, QW), F32),
            pltpu.VMEM((NG, 8, QW), F32),
            pltpu.VMEM((NG, 8, QW), F32),
            pltpu.VMEM((NG, D, OW), BF),
            pltpu.VMEM((NG, NG, 16, OW), BF),
            pltpu.VMEM((D, QW), BF),
            pltpu.VMEM((QW, DOUT), BF),
            pltpu.VMEM((D, DOUT), BF),
            pltpu.VMEM((4, 16, DOUT), BF),
            pltpu.VMEM((4, 16, DOUT), BF),
            pltpu.VMEM((4, 16, DOUT), BF),
            pltpu.VMEM((NZ, 2, DOUT), F32),
            pltpu.VMEM((NZ, 2, DOUT), F32),
            pltpu.VMEM((16, DOUT), F32),
            dma,
            dma((NG,)), dma((NG,)),
            dma, dma,
            dma((2, 8)), dma((2, 8)),
            dma((NG, NG)), dma((NG, NG)),
            dma((4,)), dma((4,)),
            dma((4,)), dma((4,)),
            dma((NZ,)), dma((NZ,)),
        ],
        compiler_params=pltpu.CompilerParams(
            collective_id=0, has_side_effects=True, vmem_limit_bytes=48 << 20
        ),
        name="tree_attention",
    )(queries, keys, values, small, out_weight)


def solution(mesh):
    in_specs = (
        P("ctx", "tp"),
        P("ctx", "tp"),
        P("ctx", "tp"),
        P("ctx"),
        P("ctx"),
        P("ctx", None),
        P("tp", None),
    )
    out_specs = P(("ctx", "tp"), None)
    return jax.shard_map(
        per_device, mesh=mesh, in_specs=in_specs, out_specs=out_specs, check_vma=False
    )
```

```python
import functools
import math

import jax
import jax.numpy as jnp
from jax import lax
from jax.experimental import pallas as pl
from jax.experimental.pallas import tpu as pltpu
from jax.sharding import PartitionSpec as P

D = 128
HEADS = 5
QW = HEADS * D
NX, NY, NZ = 4, 2, 8
NG = NX * NY
KH = 128
CUT = KH + 16
CR = CUT + KH
QR = QW + 16
OW = QW + D
DOUT = 2560
SCALE = math.log2(math.e) / math.sqrt(D)
MASKED = -1e30
START = -1e20
MESH = pl.DeviceIdType.MESH
BF = jnp.bfloat16
F32 = jnp.float32


def digits_row(high, low):
    rows = lax.broadcasted_iota(jnp.int32, (16, D), 0)
    both = jnp.where(rows == 0, jnp.broadcast_to(high, (16, D)), 0)
    both = jnp.where(rows == 1, jnp.broadcast_to(low, (16, D)), both)
    return both.astype(F32).astype(BF)


def kernel(
    q_in, k_in, v_in, e_in, p_in, r_in, w_in, out_ref,
    q_ref, k_ref, v_ref, e_ref, p_ref, r_ref,
    qt, kv, ends, stage, acc, mx, sm, osend, orecv, att, w_v, part, crecv, ysend, yrecv, zsend, zrecv, fin,
    in_sem, w_sem, qs, qr, ss, sr, rs, rr, ns, nr, os_, or_, cs, cr, ys, yr, zs, zr,
):
    c, t = lax.axis_index("ctx"), lax.axis_index("tp")
    x, y, z = c // (NY * NZ), (c // NZ) % NY, c % NZ
    g = c // NZ
    th, tc = t // 2, t % 2
    side = x // 2
    low_x = jnp.minimum(x, NX - 1 - x)
    high_x = NX - 1 - low_x

    def at(group, ring):
        return (group * NZ + ring, t)

    def remote(src, dst, send, recv, target):
        return pltpu.make_async_remote_copy(
            src_ref=src, dst_ref=dst, send_sem=send, recv_sem=recv, device_id=target, device_id_type=MESH
        )

    pairs = ((e_in, e_ref), (k_in, k_ref), (v_in, v_ref), (r_in, r_ref), (q_in, q_ref), (p_in, p_ref))
    loads = [pltpu.make_async_copy(src, dst, in_sem.at[n]) for n, (src, dst) in enumerate(pairs)]
    for load in loads:
        load.start()
    w_copy = pltpu.make_async_copy(w_in, w_v, w_sem)
    w_copy.start()

    barrier = pltpu.get_barrier_semaphore()
    for k in range(1, NG):
        pl.semaphore_signal(barrier, inc=1, device_id=at((g + k) % NG, z), device_id_type=MESH)
    for k in range(1, NZ):
        pl.semaphore_signal(barrier, inc=1, device_id=at(g, (z + k) % NZ), device_id_type=MESH)
    pl.semaphore_signal(barrier, inc=1, device_id=(c, th * 2 + 1 - tc), device_id_type=MESH)
    for k in range(1, 4):
        pl.semaphore_signal(barrier, inc=1, device_id=(c, ((th + k) % 4) * 2 + tc), device_id_type=MESH)

    for load in loads[:3]:
        load.wait()
    for half in range(2):
        keys = k_ref[half * KH : (half + 1) * KH, :]
        last_tokens = e_ref[half : half + 1, :]
        last_tokens = digits_row(last_tokens // 128, last_tokens % 128)
        turned = v_ref[half * KH : (half + 1) * KH, :].astype(F32).T.astype(BF)

        def put(ref, keys=keys, last_tokens=last_tokens, turned=turned):
            ref[0:KH, :] = keys
            ref[KH:CUT, :] = last_tokens
            ref[CUT:, :] = turned

        @pl.when(side == half)
        def _():
            put(kv.at[side, 0])

        @pl.when(side != half)
        def _():
            put(stage)

    for load in loads[3:]:
        load.wait()
    pick = lax.broadcasted_iota(jnp.int32, (D, D), 0) == jnp.broadcast_to(r_ref[...], (D, D))
    pick = jnp.where(pick, 1.0, 0.0).astype(BF)
    placed = jnp.dot(pick, q_ref[...], preferred_element_type=F32)
    for h in range(HEADS):
        qt[x, h * D : (h + 1) * D, :] = placed[:, h * D : (h + 1) * D].T.astype(BF)
    pos = p_ref[...]
    pos = digits_row(pos // 128, pos % 128)
    qt[x, QW:, :] = lax.dot_general(pos, pick, (((1,), (1,)), ((), ())), preferred_element_type=F32).astype(BF)

    pl.semaphore_wait(barrier, (NG - 1) + (NZ - 1) + 1 + 3)

    swap = remote(stage, kv.at[side, 0], ss, sr, at((NX - 1 - x) * NY + y, z))
    swap.start()

    right, left, beside = at(g, (z + 1) % NZ), at(g, (z + NZ - 1) % NZ), at(x * NY + 1 - y, z)

    def ring(e, r, step):
        lane = side if e == 0 else 1 - side
        a, b = (0, 0) if step == 1 else (2 * step - 3, 2 * step - 2)
        a, b = 2 * a + r, 2 * b + r
        n = 2 * step - 2
        sem = lambda sems, m: sems.at[e * 16 + r * 8 + m]
        if step < 4:
            to = 2 * (n + 1) + r
            return (
                remote(kv.at[lane, a], kv.at[lane, to], sem(rs, n), sem(rr, n), right),
                remote(kv.at[lane, b], kv.at[lane, to + 2], sem(rs, n + 1), sem(rr, n + 1), left),
            )
        to = 14 + r
        return (
            remote(kv.at[lane, a, 0:CUT], kv.at[lane, to, 0:CUT], sem(rs, 6), sem(rr, 6), right),
            remote(kv.at[lane, b, CUT:CR], kv.at[lane, to, CUT:CR], sem(rs, 7), sem(rr, 7), left),
        )

    def next_row(e, i):
        lane = side if e == 0 else 1 - side
        return remote(kv.at[lane, 2 * i], kv.at[lane, 2 * i + 1], ns.at[e * 3 + i], nr.at[e * 3 + i], beside)

    rings = [[{s: ring(e, r, s) for s in range(1 + r, 5)} for r in range(2)] for e in range(2)]
    sides = [[next_row(e, i) for i in range(3)] for e in range(2)]

    def launch_first(e):
        if e == 1:
            swap.wait_recv()
        for copy in rings[e][0][1]:
            copy.start()
        sides[e][0].start()

    def launch_second(e):
        for i, copy in enumerate(rings[e][0][1]):
            copy.wait_recv()
            rings[e][0][2][i].start()
            sides[e][1 + i].start()

    def launch_second_other(e):
        for i in range(2):
            sides[e][1 + i].wait_recv()
            rings[e][1][2][i].start()

    def launch_later(e, r, step):
        for i, copy in enumerate(rings[e][r][step - 1]):
            copy.wait_recv()
        for copy in rings[e][r][step]:
            copy.start()

    def query_copy(k):
        return remote(qt.at[x], qt.at[x], qs.at[k], qr.at[k], at(((x + NX - k) % NX) * NY + y, z))

    def wanted(k):
        to = (x + NX - k) % NX
        return jnp.minimum(to, NX - 1 - to) <= x

    launch_first(0)
    for k in (1, 3, 2):

        @pl.when(wanted(k))
        def _():
            query_copy(k).start()

    launch_first(1)

    acc[...] = jnp.zeros_like(acc)
    sm[...] = jnp.zeros_like(sm)
    mx[...] = jnp.full_like(mx, START)

    def slot_start(e, slot):
        i, r = slot // 2, slot % 2
        hop = (i + 1) // 2
        ring_at = (z + (NZ - hop if i % 2 else hop)) % NZ
        row = y if r == 0 else 1 - y
        group = low_x if e == 0 else high_x
        return ((group * NY + row) * NZ + ring_at) * (2 * KH) + side * KH

    def turn_ends(first, last):
        for e in range(2):
            for slot in range(first, last):
                row = kv[e, slot, KH:CUT, :].astype(F32)
                ends[e, slot] = jnp.broadcast_to(row[0:1, :] * 128.0 + row[1:2, :], (KH, KH)).T

    def flash(b, e, first, last):
        row = qt[b, QW : QW + 16, :].astype(F32)
        where = row[0:1, :] * 128.0 + row[1:2, :]
        bias, keys, turned = [], [], []
        for slot in range(first, last):
            token = (lax.broadcasted_iota(jnp.int32, (KH, D), 0) + slot_start(e, slot)).astype(F32)
            bias.append(jnp.where((token <= where) & (where < ends[e, slot]), 0.0, MASKED))
            keys.append(kv[e, slot, 0:KH, :])
            turned.append(kv[e, slot, CUT:, :])
        bias, keys, turned = jnp.concatenate(bias, 0), jnp.concatenate(keys, 0), jnp.concatenate(turned, 1)
        for h in range(HEADS):
            cols = slice(h * D, (h + 1) * D)
            s = jnp.dot(keys, qt[b, cols, :], preferred_element_type=F32) + bias
            old = mx[b, 0:1, cols]
            new = jnp.maximum(old, jnp.max(s, axis=0, keepdims=True))
            factor = jnp.exp2((old - new) * SCALE)
            p = jnp.exp2((s - new) * SCALE)
            sm[b, 0:1, cols] = sm[b, 0:1, cols] * factor + jnp.sum(p, axis=0, keepdims=True)
            o = jnp.dot(turned, p.astype(BF), preferred_element_type=F32)
            acc[b, :, cols] = acc[b, :, cols] * factor + o
            mx[b, 0:1, cols] = new

    def first_pass(n, _):
        k = n + (n // 2) * (1 - 2 * (n % 2))
        b = (x + k) % NX

        @pl.when(b >= low_x)
        def _():
            @pl.when(k > 0)
            def _():
                remote(qt.at[b], qt.at[b], qs.at[k], qr.at[k], at(b * NY + y, z)).wait_recv()

            flash(b, 0, 0, 6)

        @pl.when(b >= high_x)
        def _():
            flash(b, 1, 0, 6)

        return 0

    def middle_pass(n, _):
        b = NX - 1 - n

        @pl.when(b >= low_x)
        def _():
            flash(b, 0, 6, 10)

        @pl.when(b >= high_x)
        def _():
            flash(b, 1, 6, 10)

        return 0

    launch_second(0)
    launch_second(1)
    for e in range(2):
        sides[e][0].wait_recv()
    launch_second_other(0)
    launch_second_other(1)
    turn_ends(0, 6)
    lax.fori_loop(0, 2, first_pass, 0)
    for e in range(2):
        for r in range(2):
            launch_later(e, r, 3)
    turn_ends(6, 10)
    lax.fori_loop(2, 4, first_pass, 0)
    for e in range(2):
        for r in range(2):
            launch_later(e, r, 4)
    lax.fori_loop(0, NX, middle_pass, 0)
    for e in range(2):
        for r in range(2):
            for copy in rings[e][r][4]:
                copy.wait_recv()
    turn_ends(10, 16)

    def out_copy(b, k):
        to = (g + k) % NG
        rows = pl.ds(pl.multiple_of(to * 16, 16), 16)
        return remote(
            osend.at[b, rows], orecv.at[x, b * NY + y], os_.at[b * NG + k], or_.at[x * NG + b * NY + y], at(to, z)
        )

    def last_pass(n, _):
        b = NX - 1 - n

        @pl.when(b >= low_x)
        def _():
            flash(b, 0, 10, 16)

        @pl.when(b >= high_x)
        def _():
            flash(b, 1, 10, 16)

        @pl.when(b >= low_x)
        def _():
            stats = []
            for h in range(HEADS):
                cols = slice(h * D, (h + 1) * D)
                total = sm[b, 0:1, cols]
                some = total > 0.0
                safe = jnp.where(some, total, 1.0)
                osend[b, :, cols] = (acc[b, :, cols] / safe).T.astype(BF)
                stats.append(jnp.where(some, mx[b, 0:1, cols] * SCALE + jnp.log2(safe), START))
            lse = jnp.concatenate(stats + [jnp.zeros((8 - HEADS, D), F32)], 0)
            one = lse.astype(BF).astype(F32)
            two = (lse - one).astype(BF).astype(F32)
            three = lse - one - two
            table = jnp.concatenate([one, two, three, jnp.zeros((D - 24, D), F32)], 0)
            osend[b, :, QW:] = table.T.astype(BF)
            for k in range(1, NG):
                out_copy(b, k).start()
            orecv[x, b * NY + y] = osend[b, pl.ds(pl.multiple_of(g * 16, 16), 16), :]

        return 0

    lax.fori_loop(0, NX, last_pass, 0)

    lanes = lax.broadcasted_iota(jnp.int32, (D, QW), 0)
    heads = lax.broadcasted_iota(jnp.int32, (D, QW), 1) // D
    spread = jnp.where((lanes == heads) | (lanes == heads + 8), 1.0, 0.0).astype(BF)
    used = lax.broadcasted_iota(jnp.int32, (16, D), 1) < 8
    for b in reversed(range(NG)):
        sources = [s for s in range(NX) if min(s, NX - 1 - s) <= b // NY]
        lses = []
        for s in sources:

            @pl.when((x != s) | (y != b % NY))
            def _():
                remote(
                    orecv.at[s, b], orecv.at[s, b], os_.at[b], or_.at[s * NG + b], at(s * NY + b % NY, z)
                ).wait_recv()

            digits = orecv[s, b, :, QW:].astype(F32)
            lses.append(digits + pltpu.roll(digits, D - 8, 1) + pltpu.roll(digits, D - 16, 1))
        best = functools.reduce(jnp.maximum, lses)
        weights = [jnp.exp2(lse - best) for lse in lses]
        total = functools.reduce(jnp.add, weights)
        rows = []
        for w in weights:
            w = w / total
            high = w.astype(BF).astype(F32)
            rows.append(jnp.where(used, high, pltpu.roll(w - high, 8, 1)).astype(BF))
        wide = jnp.dot(jnp.concatenate(rows, 0), spread, preferred_element_type=F32)
        mixed = jnp.zeros((16, QW), F32)
        for n, s in enumerate(sources):
            mixed = mixed + orecv[s, b, :, 0:QW].astype(F32) * wide[n * 16 : (n + 1) * 16, :]
        att[b * 16 : (b + 1) * 16, :] = mixed.astype(BF)

    w_copy.wait()
    for n in range(DOUT // 512):
        cols = slice(n * 512, (n + 1) * 512)
        part[:, cols] = jnp.dot(att[...], w_v[:, cols], preferred_element_type=F32).astype(BF)

    def rows_of(high, core):
        return pl.ds(pl.multiple_of((high * 2 + core) * 16, 16), 16)

    core = [
        remote(part.at[rows_of(j, 1 - tc)], crecv.at[j], cs.at[j], cr.at[j], (c, th * 2 + 1 - tc)) for j in range(4)
    ]
    for copy in core:
        copy.start()
    along = []
    for j in range(4):
        core[j].wait_recv()
        both = part[rows_of(j, tc), :].astype(F32) + crecv[j].astype(F32)

        ysend[j] = both.astype(BF)

        def across(j=j):
            return remote(ysend.at[j], yrecv.at[th], ys.at[j], yr.at[th], (c, j * 2 + tc))

        along.append(across)

        @pl.when(th != j)
        def _():
            across().start()

        @pl.when(th == j)
        def _():
            yrecv[th] = both.astype(BF)

    for j in range(4):

        @pl.when(th != j)
        def _():
            remote(yrecv.at[j], yrecv.at[j], ys.at[j], yr.at[j], (c, j * 2 + tc)).wait_recv()

    total = yrecv[0].astype(F32) + yrecv[1].astype(F32) + yrecv[2].astype(F32) + yrecv[3].astype(F32)
    fin[...] = total
    for j in range(NZ):
        zsend[j] = fin[2 * j : 2 * j + 2, :]
    last = []
    for k in range(1, NZ):
        to = (z + k) % NZ
        copy = remote(zsend.at[to], zrecv.at[z], zs.at[k], zr.at[k], at(g, to))
        copy.start()
        last.append(copy)
    zrecv[z] = zsend[z]
    for copy in last:
        copy.wait_recv()
    for j in range(NZ):
        fin[2 * j : 2 * j + 2, :] = zrecv[j]
    out_ref[...] = fin[...].astype(BF)

    swap.wait_send()
    for e in range(2):
        for copy in sides[e]:
            copy.wait_send()
        for r in range(2):
            for pair in rings[e][r].values():
                for copy in pair:
                    copy.wait_send()
    for k in range(1, NX):

        @pl.when(wanted(k))
        def _():
            query_copy(k).wait_send()

    for b in range(NX):

        @pl.when(b >= low_x)
        def _():
            for k in range(1, NG):
                out_copy(b, k).wait_send()

    for copy in core:
        copy.wait_send()
    for j in range(4):

        @pl.when(th != j)
        def _():
            along[j]().wait_send()

    for copy in last:
        copy.wait_send()


def per_device(queries, keys, values, subtree_ends, query_positions, balance_route, out_weight):
    dma = pltpu.SemaphoreType.DMA
    return pl.pallas_call(
        kernel,
        out_shape=jax.ShapeDtypeStruct((16, DOUT), BF),
        in_specs=[pl.BlockSpec(memory_space=pltpu.HBM)] * 7,
        out_specs=pl.BlockSpec(memory_space=pltpu.VMEM),
        scratch_shapes=[
            pltpu.VMEM((D, QW), BF),
            pltpu.VMEM((2 * KH, D), BF),
            pltpu.VMEM((2 * KH, D), BF),
            pltpu.VMEM((2, D), jnp.int32),
            pltpu.VMEM((1, D), jnp.int32),
            pltpu.VMEM((1, D), jnp.int32),
            pltpu.VMEM((NX, QR, D), BF),
            pltpu.VMEM((2, 2 * NZ, CR, D), BF),
            pltpu.VMEM((2, 2 * NZ, KH, KH), F32),
            pltpu.VMEM((CR, D), BF),
            pltpu.VMEM((NX, D, QW), F32),
            pltpu.VMEM((NX, 8, QW), F32),
            pltpu.VMEM((NX, 8, QW), F32),
            pltpu.VMEM((NX, D, OW), BF),
            pltpu.VMEM((NX, NG, 16, OW), BF),
            pltpu.VMEM((D, QW), BF),
            pltpu.VMEM((QW, DOUT), BF),
            pltpu.VMEM((D, DOUT), BF),
            pltpu.VMEM((4, 16, DOUT), BF),
            pltpu.VMEM((4, 16, DOUT), BF),
            pltpu.VMEM((4, 16, DOUT), BF),
            pltpu.VMEM((NZ, 2, DOUT), F32),
            pltpu.VMEM((NZ, 2, DOUT), F32),
            pltpu.VMEM((16, DOUT), F32),
            dma((6,)), dma,
            dma((NX,)), dma((NX,)),
            dma, dma,
            dma((32,)), dma((32,)),
            dma((6,)), dma((6,)),
            dma((NX * NG,)), dma((NX * NG,)),
            dma((4,)), dma((4,)),
            dma((4,)), dma((4,)),
            dma((NZ,)), dma((NZ,)),
        ],
        compiler_params=pltpu.CompilerParams(
            collective_id=0, has_side_effects=True, vmem_limit_bytes=56 << 20
        ),
        name="tree_attention",
    )(
        queries, keys, values, subtree_ends.reshape(2, D), query_positions.reshape(1, D), balance_route.reshape(1, D),
        out_weight,
    )


def solution(mesh):
    in_specs = (
        P("ctx", "tp"),
        P("ctx", "tp"),
        P("ctx", "tp"),
        P("ctx"),
        P("ctx"),
        P("ctx", None),
        P("tp", None),
    )
    out_specs = P(("ctx", "tp"), None)
    return jax.shard_map(
        per_device, mesh=mesh, in_specs=in_specs, out_specs=out_specs, check_vma=False
    )
```

```python
import functools
import math

import jax
import jax.numpy as jnp
from jax import lax
from jax.experimental import pallas as pl
from jax.experimental.pallas import tpu as pltpu
from jax.sharding import PartitionSpec as P

D = 128
HEADS = 5
QW = HEADS * D
NX, NY, NZ = 4, 2, 8
NG = NX * NY
KH = 128
CUT = KH + 16
CR = CUT + KH
QR = QW + 16
OW = QW + D
DOUT = 2560
SCALE = math.log2(math.e) / math.sqrt(D)
MASKED = -1e30
START = -1e20
MESH = pl.DeviceIdType.MESH
BF = jnp.bfloat16
F32 = jnp.float32


def digits_row(high, low):
    rows = lax.broadcasted_iota(jnp.int32, (16, D), 0)
    both = jnp.where(rows == 0, jnp.broadcast_to(high, (16, D)), 0)
    both = jnp.where(rows == 1, jnp.broadcast_to(low, (16, D)), both)
    return both.astype(F32).astype(BF)


def kernel(
    q_in, k_in, v_in, e_in, p_in, r_in, w_in, out_ref,
    q_ref, k_ref, v_ref, e_ref, p_ref, r_ref,
    qz_out, qz, qt, kv, ends, stage, acc, mx, sm, osend, orecv, att, w_v, part, crecv, ysend, yall,
    in_sem, w_sem, qs, qr, ss, sr, rs, rr, ns, nr, os_, or_, cs, cr, ys, yr, zs, zr,
):
    c, t = lax.axis_index("ctx"), lax.axis_index("tp")
    x, y, z = c // (NY * NZ), (c // NZ) % NY, c % NZ
    g = c // NZ
    th, tc = t // 2, t % 2
    side = x // 2
    low_x = jnp.minimum(x, NX - 1 - x)
    high_x = NX - 1 - low_x

    def at(group, ring):
        return (group * NZ + ring, t)

    def remote(src, dst, send, recv, target):
        return pltpu.make_async_remote_copy(
            src_ref=src, dst_ref=dst, send_sem=send, recv_sem=recv, device_id=target, device_id_type=MESH
        )

    pairs = ((e_in, e_ref), (k_in, k_ref), (v_in, v_ref), (r_in, r_ref), (q_in, q_ref), (p_in, p_ref))
    loads = [pltpu.make_async_copy(src, dst, in_sem.at[n]) for n, (src, dst) in enumerate(pairs)]
    for load in loads:
        load.start()
    w_copy = pltpu.make_async_copy(w_in, w_v, w_sem)

    barrier = pltpu.get_barrier_semaphore()
    for k in range(1, NG):
        pl.semaphore_signal(barrier, inc=1, device_id=at((g + k) % NG, z), device_id_type=MESH)
    for k in range(1, NZ):
        pl.semaphore_signal(barrier, inc=1, device_id=at(g, (z + k) % NZ), device_id_type=MESH)
    pl.semaphore_signal(barrier, inc=1, device_id=(c, th * 2 + 1 - tc), device_id_type=MESH)
    for k in range(1, 4):
        pl.semaphore_signal(barrier, inc=1, device_id=(c, ((th + k) % 4) * 2 + tc), device_id_type=MESH)

    for load in loads[:3]:
        load.wait()
    for half in range(2):
        keys = k_ref[half * KH : (half + 1) * KH, :]
        last_tokens = e_ref[half : half + 1, :]
        last_tokens = digits_row(last_tokens // 128, last_tokens % 128)
        turned = v_ref[half * KH : (half + 1) * KH, :].astype(F32).T.astype(BF)

        def put(ref, keys=keys, last_tokens=last_tokens, turned=turned):
            ref[0:KH, :] = keys
            ref[KH:CUT, :] = last_tokens
            ref[CUT:, :] = turned

        @pl.when(side == half)
        def _():
            put(kv.at[side, 0])

        @pl.when(side != half)
        def _():
            put(stage)

    pl.semaphore_wait(barrier, (NG - 1) + (NZ - 1) + 1 + 3)

    swap = remote(stage, kv.at[side, 0], ss, sr, at((NX - 1 - x) * NY + y, z))
    swap.start()

    right, left, beside = at(g, (z + 1) % NZ), at(g, (z + NZ - 1) % NZ), at(x * NY + 1 - y, z)

    def ring(e, r, step):
        lane = side if e == 0 else 1 - side
        a, b = (0, 0) if step == 1 else (2 * step - 3, 2 * step - 2)
        a, b = 2 * a + r, 2 * b + r
        n = 2 * step - 2
        sem = lambda sems, m: sems.at[e * 16 + r * 8 + m]
        if step < 4:
            to = 2 * (n + 1) + r
            return (
                remote(kv.at[lane, a], kv.at[lane, to], sem(rs, n), sem(rr, n), right),
                remote(kv.at[lane, b], kv.at[lane, to + 2], sem(rs, n + 1), sem(rr, n + 1), left),
            )
        to = 14 + r
        return (
            remote(kv.at[lane, a, 0:CUT], kv.at[lane, to, 0:CUT], sem(rs, 6), sem(rr, 6), right),
            remote(kv.at[lane, b, CUT:CR], kv.at[lane, to, CUT:CR], sem(rs, 7), sem(rr, 7), left),
        )

    def next_row(e, i):
        lane = side if e == 0 else 1 - side
        return remote(kv.at[lane, 2 * i], kv.at[lane, 2 * i + 1], ns.at[e * 8 + i], nr.at[e * 8 + i], beside)

    rings = [[{s: ring(e, r, s) for s in ((1, 2, 3, 4), (3,))[r]} for r in range(2)] for e in range(2)]
    sides = [{i: next_row(e, i) for i in (0, 1, 2, 3, 4, 7)} for e in range(2)]

    def launch_first(e):
        if e == 1:
            swap.wait_recv()
        for copy in rings[e][0][1]:
            copy.start()
        sides[e][0].start()

    def launch_later(e, step):
        for i, copy in enumerate(rings[e][0][step - 1]):
            copy.wait_recv()
            rings[e][0][step][i].start()
            if 2 * step - 3 + i in sides[e]:
                sides[e][2 * step - 3 + i].start()

    def launch_other(e, step):
        for i in range(2):
            sides[e][2 * step - 3 + i].wait_recv()
            rings[e][1][step][i].start()

    def launch_last(e):
        for copy in rings[e][0][4]:
            copy.wait_recv()
        sides[e][7].start()

    def query_copy(k):
        return remote(qt.at[x], qt.at[x], qs.at[k], qr.at[k], at(((x + NX - k) % NX) * NY + y, z))

    def wanted(k):
        to = (x + NX - k) % NX
        return jnp.minimum(to, NX - 1 - to) <= x

    launch_first(0)

    for load in loads[3:]:
        load.wait()
    route = r_ref[...]
    route = (route // 2 % NZ) * 16 + (route // 16) * 2 + route % 2
    pick = lax.broadcasted_iota(jnp.int32, (D, D), 0) == jnp.broadcast_to(route, (D, D))
    pick = jnp.where(pick, 1.0, 0.0).astype(BF)
    qz_out[:, 0:QW] = jnp.dot(pick, q_ref[...], preferred_element_type=F32).astype(BF)
    pos = p_ref[...]
    rows = lax.broadcasted_iota(jnp.int32, (D, D), 0)
    pos = jnp.where(rows == 0, jnp.broadcast_to(pos // 128, (D, D)), jnp.broadcast_to(pos % 128, (D, D)))
    pos = jnp.where(rows < 2, pos, 0).astype(F32).T.astype(BF)
    qz_out[:, QW:] = jnp.dot(pick, pos, preferred_element_type=F32).astype(BF)

    def to_ring(k):
        to = (z + k) % NZ
        return remote(qz_out.at[pl.ds(pl.multiple_of(to * 16, 16), 16)], qz.at[z], zs.at[k], zr.at[k], at(g, to))

    turned_queries = [to_ring(k) for k in range(1, NZ)]
    for copy in turned_queries:
        copy.start()
    w_copy.start()
    qz[z] = qz_out[pl.ds(pl.multiple_of(z * 16, 16), 16), :]
    acc[...] = jnp.zeros_like(acc)
    sm[...] = jnp.zeros_like(sm)
    mx[...] = jnp.full_like(mx, START)
    launch_first(1)

    for copy in turned_queries:
        copy.wait_recv()
    m = lax.broadcasted_iota(jnp.int32, (D, D), 0)
    n = lax.broadcasted_iota(jnp.int32, (D, D), 1)
    order = jnp.where(n == (m // 2 % NZ) * 16 + (m // 16) * 2 + m % 2, 1.0, 0.0).astype(BF)
    placed = jnp.dot(order, qz[...].reshape(D, OW), preferred_element_type=F32)
    for h in range(HEADS):
        qt[x, h * D : (h + 1) * D, :] = placed[:, h * D : (h + 1) * D].T.astype(BF)
    qt[x, QW:, :] = placed[:, QW:].T[0:16, :].astype(BF)
    for k in (1, 3, 2):

        @pl.when(wanted(k))
        def _():
            query_copy(k).start()

    def slot_start(e, slot):
        i, r = slot // 2, slot % 2
        hop = (i + 1) // 2
        ring_at = (z + (NZ - hop if i % 2 else hop)) % NZ
        row = y if r == 0 else 1 - y
        group = low_x if e == 0 else high_x
        return ((group * NY + row) * NZ + ring_at) * (2 * KH) + side * KH

    def turn_ends(slots):
        for e in range(2):
            for slot in slots:
                row = kv[e, slot, KH:CUT, :].astype(F32)
                ends[e, slot] = jnp.broadcast_to(row[0:1, :] * 128.0 + row[1:2, :], (KH, KH)).T

    def flash(b, e, slots):
        row = qt[b, QW : QW + 16, :].astype(F32)
        where = row[0:1, :] * 128.0 + row[1:2, :]
        bias, keys, turned = [], [], []
        for slot in slots:
            token = (lax.broadcasted_iota(jnp.int32, (KH, D), 0) + slot_start(e, slot)).astype(F32)
            bias.append(jnp.where((token <= where) & (where < ends[e, slot]), 0.0, MASKED))
            keys.append(kv[e, slot, 0:KH, :])
            turned.append(kv[e, slot, CUT:, :])
        bias, keys, turned = jnp.concatenate(bias, 0), jnp.concatenate(keys, 0), jnp.concatenate(turned, 1)
        for h in range(HEADS):
            cols = slice(h * D, (h + 1) * D)
            s = jnp.dot(keys, qt[b, cols, :], preferred_element_type=F32) + bias
            old = mx[b, 0:1, cols]
            new = jnp.maximum(old, jnp.max(s, axis=0, keepdims=True))
            factor = jnp.exp2((old - new) * SCALE)
            p = jnp.exp2((s - new) * SCALE)
            sm[b, 0:1, cols] = sm[b, 0:1, cols] * factor + jnp.sum(p, axis=0, keepdims=True)
            o = jnp.dot(turned, p.astype(BF), preferred_element_type=F32)
            acc[b, :, cols] = acc[b, :, cols] * factor + o
            mx[b, 0:1, cols] = new

    def first_pass(n, _):
        k = n + (n // 2) * (1 - 2 * (n % 2))
        b = (x + k) % NX

        @pl.when(b >= low_x)
        def _():
            @pl.when(k > 0)
            def _():
                remote(qt.at[b], qt.at[b], qs.at[k], qr.at[k], at(b * NY + y, z)).wait_recv()

            flash(b, 0, range(6))

        @pl.when(b >= high_x)
        def _():
            flash(b, 1, range(6))

        return 0

    def middle_pass(slots):
        def one(n, _):
            b = NX - 1 - n

            @pl.when(b >= low_x)
            def _():
                flash(b, 0, slots)

            @pl.when(b >= high_x)
            def _():
                flash(b, 1, slots)

            return 0

        return one

    launch_later(0, 2)
    launch_later(1, 2)
    for e in range(2):
        for i in range(3):
            sides[e][i].wait_recv()
    turn_ends(range(6))
    lax.fori_loop(0, 2, first_pass, 0)
    launch_later(0, 3)
    launch_later(1, 3)
    lax.fori_loop(2, 4, first_pass, 0)
    launch_later(0, 4)
    launch_later(1, 4)
    launch_other(0, 3)
    launch_other(1, 3)
    turn_ends(range(6, 10))
    lax.fori_loop(0, 2, middle_pass(range(6, 10)), 0)
    launch_last(0)
    launch_last(1)
    lax.fori_loop(2, NX, middle_pass(range(6, 10)), 0)
    turn_ends((10, 12, 14))
    lax.fori_loop(0, NX, middle_pass((10, 12, 14)), 0)
    for e in range(2):
        for copy in rings[e][1][3]:
            copy.wait_recv()
        sides[e][7].wait_recv()
    turn_ends((11, 13, 15))

    def out_rows(group):
        return pl.ds(pl.multiple_of(group * 16, 16), 16)

    def out_copy(b, k):
        to = ((x + k // 2) % NX) * NY + (y + k % 2) % NY
        return remote(
            osend.at[b, out_rows(to)], orecv.at[x, b * NY + y], os_.at[b * NG + k], or_.at[x * NG + b * NY + y], at(to, z)
        )

    def finish(b):
        @pl.when(b >= low_x)
        def _():
            flash(b, 0, (11, 13, 15))

        @pl.when(b >= high_x)
        def _():
            flash(b, 1, (11, 13, 15))

        @pl.when(b >= low_x)
        def _():
            stats = []
            for h in range(HEADS):
                cols = slice(h * D, (h + 1) * D)
                total = sm[b, 0:1, cols]
                some = total > 0.0
                safe = jnp.where(some, total, 1.0)
                osend[b, :, cols] = (acc[b, :, cols] / safe).T.astype(BF)
                stats.append(jnp.where(some, mx[b, 0:1, cols] * SCALE + jnp.log2(safe), START))
            lse = jnp.concatenate(stats + [jnp.zeros((8 - HEADS, D), F32)], 0)
            one = lse.astype(BF).astype(F32)
            two = (lse - one).astype(BF).astype(F32)
            three = lse - one - two
            table = jnp.concatenate([one, two, three, jnp.zeros((D - 24, D), F32)], 0)
            osend[b, :, QW:] = table.T.astype(BF)
            for k in (4, 5, 2, 3, 6, 7, 1):
                out_copy(b, k).start()
            orecv[x, b * NY + y] = osend[b, pl.ds(pl.multiple_of(g * 16, 16), 16), :]

    lanes = lax.broadcasted_iota(jnp.int32, (D, QW), 0)
    heads = lax.broadcasted_iota(jnp.int32, (D, QW), 1) // D
    spread = jnp.where((lanes == heads) | (lanes == heads + 8), 1.0, 0.0).astype(BF)

    def arrive(first, last):
        for n in range(first, last):
            for s in range(NX):
                if min(s, NX - 1 - s) <= n // NY:

                    @pl.when((x != s) | (y != n % NY))
                    def _():
                        remote(
                            orecv.at[s, n], orecv.at[s, n], os_.at[n], or_.at[s * NG + n], at(s * NY + n % NY, z)
                        ).wait_recv()

    def merge(first, last, sources):
        size = (last - first) * 16
        lses = []
        for s in sources:
            digits = orecv[s, first:last, :, QW:].reshape(size, D).astype(F32)
            lses.append(digits + pltpu.roll(digits, D - 8, 1) + pltpu.roll(digits, D - 16, 1))
        best = functools.reduce(jnp.maximum, lses)
        weights = [jnp.exp2(lse - best) for lse in lses]
        total = functools.reduce(jnp.add, weights)
        used = lax.broadcasted_iota(jnp.int32, (size, D), 1) < 8
        rows = []
        for w in weights:
            w = w / total
            high = w.astype(BF).astype(F32)
            rows.append(jnp.where(used, high, pltpu.roll(w - high, 8, 1)).astype(BF))
        wide = jnp.dot(jnp.concatenate(rows, 0), spread, preferred_element_type=F32)
        mixed = jnp.zeros((size, QW), F32)
        for i, s in enumerate(sources):
            mixed = mixed + orecv[s, first:last, :, 0:QW].reshape(size, QW).astype(F32) * wide[i * size : (i + 1) * size, :]
        att[first * 16 : last * 16, :] = mixed.astype(BF)

    def core_copy(b):
        rows = pl.ds(pl.multiple_of((b * 2 + 1 - tc) * 16, 16), 16)
        return remote(part.at[rows], crecv.at[b], cs.at[b], cr.at[b], (c, th * 2 + 1 - tc))

    def project(first, last):
        rows = slice(first * 32, last * 32)
        for n in range(DOUT // 512):
            cols = slice(n * 512, (n + 1) * 512)
            part[rows, cols] = jnp.dot(att[rows, :], w_v[:, cols], preferred_element_type=F32).astype(BF)
        for b in reversed(range(first, last)):
            core_copy(b).start()

    def y_copy(b):
        return remote(ysend.at[b], yall.at[th], ys.at[b], yr.at[th], (c, b * 2 + tc))

    def share(b):
        core_copy(b).wait_recv()
        rows = pl.ds(pl.multiple_of((b * 2 + tc) * 16, 16), 16)
        both = (part[rows, :].astype(F32) + crecv[b].astype(F32)).astype(BF)

        @pl.when(th != b)
        def _():
            ysend[b] = both
            y_copy(b).start()

        @pl.when(th == b)
        def _():
            yall[th] = both

    for b in reversed(range(NX)):
        finish(b)
    w_copy.wait()
    swap.wait_send()
    for e in range(2):
        for copy in sides[e].values():
            copy.wait_send()
        for r in range(2):
            for pair in rings[e][r].values():
                for copy in pair:
                    copy.wait_send()
    for k in range(1, NX):

        @pl.when(wanted(k))
        def _():
            query_copy(k).wait_send()

    for copy in turned_queries:
        copy.wait_send()
    arrive(4, 8)
    merge(4, 8, (0, 1, 2, 3))
    project(2, 4)
    share(3)
    share(2)
    arrive(0, 4)
    merge(2, 4, (0, 1, 2, 3))
    merge(0, 2, (0, 3))
    project(0, 2)
    share(1)
    share(0)
    for b in range(NX):

        @pl.when(b >= low_x)
        def _():
            for k in range(1, NG):
                out_copy(b, k).wait_send()

    for j in range(4):

        @pl.when(th != j)
        def _():
            remote(yall.at[j], yall.at[j], ys.at[j], yr.at[j], (c, j * 2 + tc)).wait_recv()

    out_ref[...] = (yall[0].astype(F32) + yall[1].astype(F32) + yall[2].astype(F32) + yall[3].astype(F32)).astype(BF)

    for b in range(NX):
        core_copy(b).wait_send()

        @pl.when(th != b)
        def _():
            y_copy(b).wait_send()


def per_device(queries, keys, values, subtree_ends, query_positions, balance_route, out_weight):
    dma = pltpu.SemaphoreType.DMA
    return pl.pallas_call(
        kernel,
        out_shape=jax.ShapeDtypeStruct((16, DOUT), BF),
        in_specs=[pl.BlockSpec(memory_space=pltpu.HBM)] * 7,
        out_specs=pl.BlockSpec(memory_space=pltpu.VMEM),
        scratch_shapes=[
            pltpu.VMEM((D, QW), BF),
            pltpu.VMEM((2 * KH, D), BF),
            pltpu.VMEM((2 * KH, D), BF),
            pltpu.VMEM((2, D), jnp.int32),
            pltpu.VMEM((1, D), jnp.int32),
            pltpu.VMEM((1, D), jnp.int32),
            pltpu.VMEM((D, OW), BF),
            pltpu.VMEM((NZ, 16, OW), BF),
            pltpu.VMEM((NX, QR, D), BF),
            pltpu.VMEM((2, 2 * NZ, CR, D), BF),
            pltpu.VMEM((2, 2 * NZ, KH, KH), F32),
            pltpu.VMEM((CR, D), BF),
            pltpu.VMEM((NX, D, QW), F32),
            pltpu.VMEM((NX, 8, QW), F32),
            pltpu.VMEM((NX, 8, QW), F32),
            pltpu.VMEM((NX, D, OW), BF),
            pltpu.VMEM((NX, NG, 16, OW), BF),
            pltpu.VMEM((D, QW), BF),
            pltpu.VMEM((QW, DOUT), BF),
            pltpu.VMEM((D, DOUT), BF),
            pltpu.VMEM((4, 16, DOUT), BF),
            pltpu.VMEM((4, 16, DOUT), BF),
            pltpu.VMEM((4, 16, DOUT), BF),
            dma((6,)), dma,
            dma((NX,)), dma((NX,)),
            dma, dma,
            dma((32,)), dma((32,)),
            dma((16,)), dma((16,)),
            dma((NX * NG,)), dma((NX * NG,)),
            dma((4,)), dma((4,)),
            dma((4,)), dma((4,)),
            dma((NZ,)), dma((NZ,)),
        ],
        compiler_params=pltpu.CompilerParams(
            collective_id=0, has_side_effects=True, vmem_limit_bytes=56 << 20
        ),
        name="tree_attention",
    )(
        queries, keys, values, subtree_ends.reshape(2, D), query_positions.reshape(1, D), balance_route.reshape(1, D),
        out_weight,
    )


def solution(mesh):
    in_specs = (
        P("ctx", "tp"),
        P("ctx", "tp"),
        P("ctx", "tp"),
        P("ctx"),
        P("ctx"),
        P("ctx", None),
        P("tp", None),
    )
    out_specs = P(("ctx", "tp"), None)
    return jax.shard_map(
        per_device, mesh=mesh, in_specs=in_specs, out_specs=out_specs, check_vma=False
    )
```

```python
import functools
import math

import jax
import jax.numpy as jnp
from jax import lax
from jax.experimental import pallas as pl
from jax.experimental.pallas import tpu as pltpu
from jax.sharding import PartitionSpec as P

D = 128
HEADS = 5
QW = HEADS * D
NX, NY, NZ = 4, 2, 8
NG = NX * NY
KH = 128
CUT = KH + 16
CR = CUT + KH
QR = QW + 16
OW = QW + D
DOUT = 2560
SCALE = math.log2(math.e) / math.sqrt(D)
MASKED = -1e30
START = -1e20
MESH = pl.DeviceIdType.MESH
BF = jnp.bfloat16
F32 = jnp.float32


def digits_row(high, low):
    rows = lax.broadcasted_iota(jnp.int32, (16, D), 0)
    both = jnp.where(rows == 0, jnp.broadcast_to(high, (16, D)), 0)
    both = jnp.where(rows == 1, jnp.broadcast_to(low, (16, D)), both)
    return both.astype(F32).astype(BF)


def kernel(
    q_in, k_in, v_in, e_in, p_in, r_in, w_in, out_ref,
    q_ref, k_ref, v_ref, e_ref, p_ref, r_ref,
    qz_out, qz, qt, kv, ends, stage, acc, mx, sm, osend, orecv, att, w_v, part, crecv, ysend, yall,
    in_sem, w_sem, qs, qr, ss, sr, rs, rr, ns, nr, os_, or_, cs, cr, ys, yr, zs, zr,
):
    c, t = lax.axis_index("ctx"), lax.axis_index("tp")
    x, y, z = c // (NY * NZ), (c // NZ) % NY, c % NZ
    g = c // NZ
    th, tc = t // 2, t % 2
    side = x // 2
    low_x = jnp.minimum(x, NX - 1 - x)
    high_x = NX - 1 - low_x

    def at(group, ring):
        return (group * NZ + ring, t)

    def remote(src, dst, send, recv, target):
        return pltpu.make_async_remote_copy(
            src_ref=src, dst_ref=dst, send_sem=send, recv_sem=recv, device_id=target, device_id_type=MESH
        )

    pairs = ((e_in, e_ref), (k_in, k_ref), (v_in, v_ref), (r_in, r_ref), (q_in, q_ref), (p_in, p_ref))
    loads = [pltpu.make_async_copy(src, dst, in_sem.at[n]) for n, (src, dst) in enumerate(pairs)]
    for load in loads:
        load.start()
    w_copy = pltpu.make_async_copy(w_in, w_v, w_sem)

    barrier = pltpu.get_barrier_semaphore()
    for k in range(1, NG):
        pl.semaphore_signal(barrier, inc=1, device_id=at((g + k) % NG, z), device_id_type=MESH)
    for k in range(1, NZ):
        pl.semaphore_signal(barrier, inc=1, device_id=at(g, (z + k) % NZ), device_id_type=MESH)
    pl.semaphore_signal(barrier, inc=1, device_id=(c, th * 2 + 1 - tc), device_id_type=MESH)
    for k in range(1, 4):
        pl.semaphore_signal(barrier, inc=1, device_id=(c, ((th + k) % 4) * 2 + tc), device_id_type=MESH)

    for load in loads[:3]:
        load.wait()
    for half in range(2):
        keys = k_ref[half * KH : (half + 1) * KH, :]
        last_tokens = e_ref[half : half + 1, :]
        last_tokens = digits_row(last_tokens // 128, last_tokens % 128)
        turned = v_ref[half * KH : (half + 1) * KH, :].astype(F32).T.astype(BF)

        def put(ref, keys=keys, last_tokens=last_tokens, turned=turned):
            ref[0:KH, :] = keys
            ref[KH:CUT, :] = last_tokens
            ref[CUT:, :] = turned

        @pl.when(side == half)
        def _():
            put(kv.at[side, 0])

        @pl.when(side != half)
        def _():
            put(stage)

    pl.semaphore_wait(barrier, (NG - 1) + (NZ - 1) + 1 + 3)

    swap = remote(stage, kv.at[side, 0], ss, sr, at((NX - 1 - x) * NY + y, z))
    swap.start()

    right, left, beside = at(g, (z + 1) % NZ), at(g, (z + NZ - 1) % NZ), at(x * NY + 1 - y, z)

    def ring(e, r, step):
        lane = side if e == 0 else 1 - side
        a, b = (0, 0) if step == 1 else (2 * step - 3, 2 * step - 2)
        a, b = 2 * a + r, 2 * b + r
        n = 2 * step - 2
        sem = lambda sems, m: sems.at[e * 16 + r * 8 + m]
        if step < 4:
            to = 2 * (n + 1) + r
            return (
                remote(kv.at[lane, a], kv.at[lane, to], sem(rs, n), sem(rr, n), right),
                remote(kv.at[lane, b], kv.at[lane, to + 2], sem(rs, n + 1), sem(rr, n + 1), left),
            )
        to = 14 + r
        return (
            remote(kv.at[lane, a, 0:CUT], kv.at[lane, to, 0:CUT], sem(rs, 6), sem(rr, 6), right),
            remote(kv.at[lane, b, CUT:CR], kv.at[lane, to, CUT:CR], sem(rs, 7), sem(rr, 7), left),
        )

    def next_row(e, i):
        lane = side if e == 0 else 1 - side
        return remote(kv.at[lane, 2 * i], kv.at[lane, 2 * i + 1], ns.at[e * 8 + i], nr.at[e * 8 + i], beside)

    rings = [[{s: ring(e, r, s) for s in ((1, 2, 3, 4), (3,))[r]} for r in range(2)] for e in range(2)]
    sides = [{i: next_row(e, i) for i in (0, 1, 2, 3, 4, 7)} for e in range(2)]

    def launch_first(e):
        if e == 1:
            swap.wait_recv()
        for copy in rings[e][0][1]:
            copy.start()
        sides[e][0].start()

    def launch_later(e, step):
        for i, copy in enumerate(rings[e][0][step - 1]):
            copy.wait_recv()
            rings[e][0][step][i].start()
            if 2 * step - 3 + i in sides[e]:
                sides[e][2 * step - 3 + i].start()

    def launch_other(e, step):
        for i in range(2):
            sides[e][2 * step - 3 + i].wait_recv()
            rings[e][1][step][i].start()

    def launch_last(e):
        for copy in rings[e][0][4]:
            copy.wait_recv()
        sides[e][7].start()

    def query_copy(k):
        return remote(qt.at[x], qt.at[x], qs.at[k], qr.at[k], at(((x + NX - k) % NX) * NY + y, z))

    def wanted(k):
        to = (x + NX - k) % NX
        return jnp.minimum(to, NX - 1 - to) <= x

    launch_first(0)

    for load in loads[3:]:
        load.wait()
    route = r_ref[...]
    route = (route // 2 % NZ) * 16 + (route // 16) * 2 + route % 2
    pick = lax.broadcasted_iota(jnp.int32, (D, D), 0) == jnp.broadcast_to(route, (D, D))
    pick = jnp.where(pick, 1.0, 0.0).astype(BF)
    qz_out[:, 0:QW] = jnp.dot(pick, q_ref[...], preferred_element_type=F32).astype(BF)
    pos = p_ref[...]
    rows = lax.broadcasted_iota(jnp.int32, (D, D), 0)
    pos = jnp.where(rows == 0, jnp.broadcast_to(pos // 128, (D, D)), jnp.broadcast_to(pos % 128, (D, D)))
    pos = jnp.where(rows < 2, pos, 0).astype(F32).T.astype(BF)
    qz_out[:, QW:] = jnp.dot(pick, pos, preferred_element_type=F32).astype(BF)

    def to_ring(k):
        to = (z + k) % NZ
        return remote(qz_out.at[pl.ds(pl.multiple_of(to * 16, 16), 16)], qz.at[z], zs.at[k], zr.at[k], at(g, to))

    turned_queries = [to_ring(k) for k in range(1, NZ)]
    for copy in turned_queries:
        copy.start()
    w_copy.start()
    qz[z] = qz_out[pl.ds(pl.multiple_of(z * 16, 16), 16), :]
    acc[...] = jnp.zeros_like(acc)
    sm[...] = jnp.zeros_like(sm)
    mx[...] = jnp.full_like(mx, START)
    launch_first(1)

    for copy in turned_queries:
        copy.wait_recv()
    m = lax.broadcasted_iota(jnp.int32, (D, D), 0)
    n = lax.broadcasted_iota(jnp.int32, (D, D), 1)
    order = jnp.where(n == (m // 2 % NZ) * 16 + (m // 16) * 2 + m % 2, 1.0, 0.0).astype(BF)
    placed = jnp.dot(order, qz[...].reshape(D, OW), preferred_element_type=F32)
    for h in range(HEADS):
        qt[x, h * D : (h + 1) * D, :] = placed[:, h * D : (h + 1) * D].T.astype(BF)
    qt[x, QW:, :] = placed[:, QW:].T[0:16, :].astype(BF)
    for k in (1, 3, 2):

        @pl.when(wanted(k))
        def _():
            query_copy(k).start()

    def slot_start(e, slot):
        i, r = slot // 2, slot % 2
        hop = (i + 1) // 2
        ring_at = (z + (NZ - hop if i % 2 else hop)) % NZ
        row = y if r == 0 else 1 - y
        group = low_x if e == 0 else high_x
        return ((group * NY + row) * NZ + ring_at) * (2 * KH) + side * KH

    def turn_ends(slots):
        for e in range(2):
            for slot in slots:
                row = kv[e, slot, KH:CUT, :].astype(F32)
                ends[e, slot] = jnp.broadcast_to(row[0:1, :] * 128.0 + row[1:2, :], (KH, KH)).T

    def flash(b, e, slots):
        row = qt[b, QW : QW + 16, :].astype(F32)
        where = row[0:1, :] * 128.0 + row[1:2, :]
        bias, keys, turned = [], [], []
        for slot in slots:
            token = (lax.broadcasted_iota(jnp.int32, (KH, D), 0) + slot_start(e, slot)).astype(F32)
            bias.append(jnp.where((token <= where) & (where < ends[e, slot]), 0.0, MASKED))
            keys.append(kv[e, slot, 0:KH, :])
            turned.append(kv[e, slot, CUT:, :])
        bias, keys, turned = jnp.concatenate(bias, 0), jnp.concatenate(keys, 0), jnp.concatenate(turned, 1)
        for h in range(HEADS):
            cols = slice(h * D, (h + 1) * D)
            s = jnp.dot(keys, qt[b, cols, :], preferred_element_type=F32) + bias
            old = mx[b, 0:1, cols]
            new = jnp.maximum(old, jnp.max(s, axis=0, keepdims=True))
            factor = jnp.exp2((old - new) * SCALE)
            p = jnp.exp2((s - new) * SCALE)
            sm[b, 0:1, cols] = sm[b, 0:1, cols] * factor + jnp.sum(p, axis=0, keepdims=True)
            o = jnp.dot(turned, p.astype(BF), preferred_element_type=F32)
            acc[b, :, cols] = acc[b, :, cols] * factor + o
            mx[b, 0:1, cols] = new

    def first_pass(n, _):
        k = n + (n // 2) * (1 - 2 * (n % 2))
        b = (x + k) % NX

        @pl.when(b >= low_x)
        def _():
            @pl.when(k > 0)
            def _():
                remote(qt.at[b], qt.at[b], qs.at[k], qr.at[k], at(b * NY + y, z)).wait_recv()

            flash(b, 0, (0, 2, 4))

        @pl.when(b >= high_x)
        def _():
            flash(b, 1, (0, 2, 4))

        return 0

    def middle_pass(slots):
        def one(n, _):
            b = NX - 1 - n

            @pl.when(b >= low_x)
            def _():
                flash(b, 0, slots)

            @pl.when(b >= high_x)
            def _():
                flash(b, 1, slots)

            return 0

        return one

    launch_later(0, 2)
    launch_later(1, 2)
    turn_ends((0, 2, 4))
    lax.fori_loop(0, 2, first_pass, 0)
    launch_later(0, 3)
    launch_later(1, 3)
    lax.fori_loop(2, NX, first_pass, 0)
    for e in range(2):
        for i in range(3):
            sides[e][i].wait_recv()
    turn_ends((1, 3, 5))
    lax.fori_loop(0, 2, middle_pass((1, 3, 5)), 0)
    launch_later(0, 4)
    launch_later(1, 4)
    lax.fori_loop(2, NX, middle_pass((1, 3, 5)), 0)
    launch_other(0, 3)
    launch_other(1, 3)
    turn_ends((6, 8, 10, 12))
    lax.fori_loop(0, 2, middle_pass((6, 8, 10, 12)), 0)
    launch_last(0)
    launch_last(1)
    lax.fori_loop(2, NX, middle_pass((6, 8, 10, 12)), 0)
    turn_ends((7, 9, 14))
    lax.fori_loop(0, NX, middle_pass((7, 9, 14)), 0)
    for e in range(2):
        for copy in rings[e][1][3]:
            copy.wait_recv()
        sides[e][7].wait_recv()
    turn_ends((11, 13, 15))

    def out_rows(group):
        return pl.ds(pl.multiple_of(group * 16, 16), 16)

    def out_copy(b, k):
        to = ((x + k // 2) % NX) * NY + (y + k % 2) % NY
        return remote(
            osend.at[b, out_rows(to)], orecv.at[x, b * NY + y], os_.at[b * NG + k], or_.at[x * NG + b * NY + y], at(to, z)
        )

    def finish(b):
        @pl.when(b >= low_x)
        def _():
            flash(b, 0, (11, 13, 15))

        @pl.when(b >= high_x)
        def _():
            flash(b, 1, (11, 13, 15))

        @pl.when(b >= low_x)
        def _():
            stats = []
            for h in range(HEADS):
                cols = slice(h * D, (h + 1) * D)
                total = sm[b, 0:1, cols]
                some = total > 0.0
                safe = jnp.where(some, total, 1.0)
                osend[b, :, cols] = (acc[b, :, cols] / safe).T.astype(BF)
                stats.append(jnp.where(some, mx[b, 0:1, cols] * SCALE + jnp.log2(safe), START))
            lse = jnp.concatenate(stats + [jnp.zeros((8 - HEADS, D), F32)], 0)
            one = lse.astype(BF).astype(F32)
            two = (lse - one).astype(BF).astype(F32)
            three = lse - one - two
            table = jnp.concatenate([one, two, three, jnp.zeros((D - 24, D), F32)], 0)
            osend[b, :, QW:] = table.T.astype(BF)
            for k in (4, 5, 2, 3, 6, 7, 1):
                out_copy(b, k).start()
            orecv[x, b * NY + y] = osend[b, pl.ds(pl.multiple_of(g * 16, 16), 16), :]

    lanes = lax.broadcasted_iota(jnp.int32, (D, QW), 0)
    heads = lax.broadcasted_iota(jnp.int32, (D, QW), 1) // D
    spread = jnp.where((lanes == heads) | (lanes == heads + 8), 1.0, 0.0).astype(BF)

    def arrive(first, last):
        for n in range(first, last):
            for s in range(NX):
                if min(s, NX - 1 - s) <= n // NY:

                    @pl.when((x != s) | (y != n % NY))
                    def _():
                        remote(
                            orecv.at[s, n], orecv.at[s, n], os_.at[n], or_.at[s * NG + n], at(s * NY + n % NY, z)
                        ).wait_recv()

    def merge(first, last, sources):
        size = (last - first) * 16
        lses = []
        for s in sources:
            digits = orecv[s, first:last, :, QW:].reshape(size, D).astype(F32)
            lses.append(digits + pltpu.roll(digits, D - 8, 1) + pltpu.roll(digits, D - 16, 1))
        best = functools.reduce(jnp.maximum, lses)
        weights = [jnp.exp2(lse - best) for lse in lses]
        total = functools.reduce(jnp.add, weights)
        used = lax.broadcasted_iota(jnp.int32, (size, D), 1) < 8
        rows = []
        for w in weights:
            w = w / total
            high = w.astype(BF).astype(F32)
            rows.append(jnp.where(used, high, pltpu.roll(w - high, 8, 1)).astype(BF))
        wide = jnp.dot(jnp.concatenate(rows, 0), spread, preferred_element_type=F32)
        mixed = jnp.zeros((size, QW), F32)
        for i, s in enumerate(sources):
            mixed = mixed + orecv[s, first:last, :, 0:QW].reshape(size, QW).astype(F32) * wide[i * size : (i + 1) * size, :]
        att[first * 16 : last * 16, :] = mixed.astype(BF)

    def core_copy(b):
        rows = pl.ds(pl.multiple_of((b * 2 + 1 - tc) * 16, 16), 16)
        return remote(part.at[rows], crecv.at[b], cs.at[b], cr.at[b], (c, th * 2 + 1 - tc))

    def project(first, last):
        rows = slice(first * 32, last * 32)
        for n in range(DOUT // 512):
            cols = slice(n * 512, (n + 1) * 512)
            part[rows, cols] = jnp.dot(att[rows, :], w_v[:, cols], preferred_element_type=F32).astype(BF)
        for b in reversed(range(first, last)):
            core_copy(b).start()

    def y_copy(b):
        return remote(ysend.at[b], yall.at[th], ys.at[b], yr.at[th], (c, b * 2 + tc))

    def share(b):
        core_copy(b).wait_recv()
        rows = pl.ds(pl.multiple_of((b * 2 + tc) * 16, 16), 16)
        both = (part[rows, :].astype(F32) + crecv[b].astype(F32)).astype(BF)

        @pl.when(th != b)
        def _():
            ysend[b] = both
            y_copy(b).start()

        @pl.when(th == b)
        def _():
            yall[th] = both

    def last_pass(n, _):
        finish(NX - 1 - n)
        return 0

    lax.fori_loop(0, NX, last_pass, 0)
    w_copy.wait()
    swap.wait_send()
    for e in range(2):
        for copy in sides[e].values():
            copy.wait_send()
        for r in range(2):
            for pair in rings[e][r].values():
                for copy in pair:
                    copy.wait_send()
    for k in range(1, NX):

        @pl.when(wanted(k))
        def _():
            query_copy(k).wait_send()

    for copy in turned_queries:
        copy.wait_send()
    arrive(4, 8)
    merge(4, 8, (0, 1, 2, 3))
    project(2, 4)
    share(3)
    share(2)
    arrive(0, 4)
    merge(2, 4, (0, 1, 2, 3))
    merge(0, 2, (0, 3))
    project(0, 2)
    share(1)
    share(0)
    for b in range(NX):

        @pl.when(b >= low_x)
        def _():
            for k in range(1, NG):
                out_copy(b, k).wait_send()

    for j in range(4):

        @pl.when(th != j)
        def _():
            remote(yall.at[j], yall.at[j], ys.at[j], yr.at[j], (c, j * 2 + tc)).wait_recv()

    out_ref[...] = (yall[0].astype(F32) + yall[1].astype(F32) + yall[2].astype(F32) + yall[3].astype(F32)).astype(BF)

    for b in range(NX):
        core_copy(b).wait_send()

        @pl.when(th != b)
        def _():
            y_copy(b).wait_send()


def per_device(queries, keys, values, subtree_ends, query_positions, balance_route, out_weight):
    dma = pltpu.SemaphoreType.DMA
    return pl.pallas_call(
        kernel,
        out_shape=jax.ShapeDtypeStruct((16, DOUT), BF),
        in_specs=[pl.BlockSpec(memory_space=pltpu.HBM)] * 7,
        out_specs=pl.BlockSpec(memory_space=pltpu.VMEM),
        scratch_shapes=[
            pltpu.VMEM((D, QW), BF),
            pltpu.VMEM((2 * KH, D), BF),
            pltpu.VMEM((2 * KH, D), BF),
            pltpu.VMEM((2, D), jnp.int32),
            pltpu.VMEM((1, D), jnp.int32),
            pltpu.VMEM((1, D), jnp.int32),
            pltpu.VMEM((D, OW), BF),
            pltpu.VMEM((NZ, 16, OW), BF),
            pltpu.VMEM((NX, QR, D), BF),
            pltpu.VMEM((2, 2 * NZ, CR, D), BF),
            pltpu.VMEM((2, 2 * NZ, KH, KH), F32),
            pltpu.VMEM((CR, D), BF),
            pltpu.VMEM((NX, D, QW), F32),
            pltpu.VMEM((NX, 8, QW), F32),
            pltpu.VMEM((NX, 8, QW), F32),
            pltpu.VMEM((NX, D, OW), BF),
            pltpu.VMEM((NX, NG, 16, OW), BF),
            pltpu.VMEM((D, QW), BF),
            pltpu.VMEM((QW, DOUT), BF),
            pltpu.VMEM((D, DOUT), BF),
            pltpu.VMEM((4, 16, DOUT), BF),
            pltpu.VMEM((4, 16, DOUT), BF),
            pltpu.VMEM((4, 16, DOUT), BF),
            dma((6,)), dma,
            dma((NX,)), dma((NX,)),
            dma, dma,
            dma((32,)), dma((32,)),
            dma((16,)), dma((16,)),
            dma((NX * NG,)), dma((NX * NG,)),
            dma((4,)), dma((4,)),
            dma((4,)), dma((4,)),
            dma((NZ,)), dma((NZ,)),
        ],
        compiler_params=pltpu.CompilerParams(
            collective_id=0, has_side_effects=True, vmem_limit_bytes=56 << 20
        ),
        name="tree_attention",
    )(
        queries, keys, values, subtree_ends.reshape(2, D), query_positions.reshape(1, D), balance_route.reshape(1, D),
        out_weight,
    )


def solution(mesh):
    in_specs = (
        P("ctx", "tp"),
        P("ctx", "tp"),
        P("ctx", "tp"),
        P("ctx"),
        P("ctx"),
        P("ctx", None),
        P("tp", None),
    )
    out_specs = P(("ctx", "tp"), None)
    return jax.shard_map(
        per_device, mesh=mesh, in_specs=in_specs, out_specs=out_specs, check_vma=False
    )
```
